128 devices in a mesh: seq: 32 (over z_lo, y, x), head: 4 (over z_hi, core).
Axes of the slice: x: 4, y: 4, z: 4 (z_hi: 2, z_lo: 2; z = z_hi * 2 + z_lo), core: 2. Of those that a mesh axis runs over, the one named last changes fastest.
Arguments:
- query: bfloat16 [4096, 96, 128], P(('seq', 'head')), may hold values from -15.6 to 15.6
- key_new: bfloat16 [4096, 8, 128], P('seq', 'head'), may hold values from -6 to 6
- value_new: bfloat16 [4096, 8, 128], P('seq', 'head'), may hold values from -6 to 6
- key_old: bfloat16 [4096, 8, 128], P('seq', 'head'), may hold values from -6 to 6
- value_old: bfloat16 [4096, 8, 128], P('seq', 'head'), may hold values from -6 to 6
- offset: int32 [1], replicated, may hold values from 0 to 4095
- windows: int32 [8], P('head'), may hold values from 2048 to 4096, as said below
- grad_out: bfloat16 [4096, 96, 128], P(('seq', 'head')), may hold values from -6 to 6
Outputs:
- grad_query: float32 [4096, 96, 128], P(('seq', 'head'))
- grad_key_new: float32 [4096, 8, 128], P('seq', 'head')
- grad_value_new: float32 [4096, 8, 128], P('seq', 'head')
- grad_key_old: float32 [4096, 8, 128], P('seq', 'head')
- grad_value_old: float32 [4096, 8, 128], P('seq', 'head')
The draws below stay inside these ranges and needn't reach their ends.
Inputs may be any that keep to these rules, and one draw needn't show every extreme that they name: `windows`: one key-value head has a window of exactly 4096 tokens and another of exactly 2048.
All inputs are finite; a program needn't handle non-finite values.
Results may differ from the reference program's by a relative error of at most 0.003.
Values may be sent and summed in bfloat16 or wider, within the bound.
No kernel may reach another device: no remote copies, remote signals or barrier semaphores. Data moves between devices by JAX's collectives and lax.ppermute only.
A program may use at most 128 MiB of HBM per device.

```python
import math
import jax
import jax.numpy as jnp
from jax import lax

HQ = 96
KVH = 8
HD = 128
GROUP = 12
STRETCH = 4096


def draw_query(key, part):
    values = jax.random.truncated_normal(jax.random.fold_in(key, 23), -6.0, 6.0, (STRETCH, HQ, HD), jnp.float32)
    return values.astype(jnp.bfloat16)


def draw_key_new(key, part):
    values = jax.random.truncated_normal(jax.random.fold_in(key, 33), -6.0, 6.0, (STRETCH, KVH, HD), jnp.float32)
    return values.astype(jnp.bfloat16)


def draw_windows(key, part):
    picks = jax.random.randint(jax.random.fold_in(key, 41), (KVH,), STRETCH // 2, STRETCH + 1)
    order = jax.random.permutation(jax.random.fold_in(key, 42), KVH)
    places = jnp.arange(KVH)
    picks = jnp.where(places == order[0], STRETCH, picks)
    picks = jnp.where(places == order[1], STRETCH // 2, picks)
    return picks.astype(jnp.int32)


def shard_levels(rng, dims, split, least, top_value):
    gain, own = 1.0, jax.random.fold_in(rng, 6)
    for position, shards_of in split:
        heights = jnp.exp(jax.random.uniform(jax.random.fold_in(own, position), (shards_of,), jnp.float32, least / len(split), top_value / len(split)))
        gain = gain * jnp.repeat(heights, dims[position] // shards_of).reshape([-1 if axis == position else 1 for axis in range(len(dims))])
    return gain


def normal_values(key, extent, scale, most, pieces=(), held_as=jnp.bfloat16):
    values = jax.random.normal(key, extent, jnp.float32) * scale
    if len(pieces) > 0:
        values = shard_levels(key, extent, pieces, -0.22, 0.18) * values
    return jnp.clip(values, min=-most, max=most).astype(held_as)


def setup_inputs(seed: int = 0) -> dict:
    key_of = jax.random.split(jax.random.key(seed), 9)
    query = draw_query(jax.random.fold_in(key_of[8], 71), 0)
    key_new = draw_key_new(jax.random.fold_in(key_of[8], 71), 0)
    value_new = normal_values(key_of[2], (STRETCH, KVH, HD), 1.0, 6.0, ((0, 32), (1, 4)))
    key_old = normal_values(key_of[3], (STRETCH, KVH, HD), 1.0, 6.0, ((0, 32), (1, 4)))
    value_old = normal_values(key_of[4], (STRETCH, KVH, HD), 1.0, 6.0, ((0, 32), (1, 4)))
    offset = jax.random.randint(key_of[5], (1,), 0, STRETCH).astype(jnp.int32)
    windows = draw_windows(jax.random.fold_in(key_of[8], 71), 0)
    grad_out = normal_values(key_of[7], (STRETCH, HQ, HD), 1.0, 6.0, ((0, 128),))
    return {"query": query, "key_new": key_new, "value_new": value_new, "key_old": key_old, "value_old": value_old, "offset": offset, "windows": windows, "grad_out": grad_out}


def reference(query, key_new, value_new, key_old, value_old, offset, windows, grad_out):
    score_scale = 1.0 / math.sqrt(HD)
    slot_order = (jnp.arange(STRETCH, dtype=jnp.int32) + offset[0]) % STRETCH
    all_keys = jnp.concatenate([key_old[slot_order], key_new], axis=0)
    all_values = jnp.concatenate([value_old[slot_order], value_new], axis=0)
    row_block = math.gcd(STRETCH, 128)
    key_span = STRETCH + row_block
    block_starts = jnp.arange(STRETCH // row_block, dtype=jnp.int32) * row_block

    def visit_block(state_in, row_start):
        key_grads, value_grads = state_in
        queries = lax.dynamic_slice_in_dim(query, row_start, row_block, 0).astype(jnp.float32).reshape(row_block, KVH, GROUP, HD)
        out_grads = lax.dynamic_slice_in_dim(grad_out, row_start, row_block, 0).astype(jnp.float32).reshape(row_block, KVH, GROUP, HD)
        key_rows = lax.dynamic_slice_in_dim(all_keys, row_start, key_span, 0).astype(jnp.float32)
        value_rows = lax.dynamic_slice_in_dim(all_values, row_start, key_span, 0).astype(jnp.float32)
        query_pos = row_start + jnp.arange(row_block, dtype=jnp.int32)
        key_pos = row_start + jnp.arange(key_span, dtype=jnp.int32) - STRETCH
        key_row = key_pos[None, None, None, :]
        query_col = query_pos[:, None, None, None]
        seen = (key_row <= query_col) & (key_row > query_col - windows[None, :, None, None])
        scores = score_scale * jnp.einsum('qgjd,kgd->qgjk', queries, key_rows)
        masked = jnp.where(seen, scores, -jnp.inf)
        row_top = lax.optimization_barrier(jnp.max(masked, axis=-1, keepdims=True))
        log_total = row_top + jnp.log(lax.optimization_barrier(jnp.sum(jnp.exp(masked - row_top), axis=-1, keepdims=True)))
        weights = jnp.where(seen, jnp.exp(scores - log_total), 0.0)
        weight_grad = jnp.einsum('qgjd,kgd->qgjk', out_grads, value_rows)
        row_delta = lax.optimization_barrier(jnp.sum(weights * weight_grad, axis=-1, keepdims=True))
        dscore = lax.optimization_barrier((weights * (weight_grad - row_delta)).astype(jnp.bfloat16)).astype(jnp.float32)
        weights_low = lax.optimization_barrier(weights.astype(jnp.bfloat16)).astype(jnp.float32)
        query_grad = score_scale * jnp.einsum('qgjk,kgd->qgjd', dscore, key_rows)
        key_part = score_scale * jnp.einsum('qgjk,qgjd->kgd', dscore, queries)
        value_part = jnp.einsum('qgjk,qgjd->kgd', weights_low, out_grads)
        key_grads = lax.dynamic_update_slice_in_dim(key_grads, lax.dynamic_slice_in_dim(key_grads, row_start, key_span, 0) + key_part, row_start, 0)
        value_grads = lax.dynamic_update_slice_in_dim(value_grads, lax.dynamic_slice_in_dim(value_grads, row_start, key_span, 0) + value_part, row_start, 0)
        return ((key_grads, value_grads), query_grad.reshape(row_block, HQ, HD))
    zero_grads = jnp.zeros((2 * STRETCH, KVH, HD), jnp.float32)
    final_state, query_blocks = lax.scan(visit_block, (zero_grads, zero_grads), block_starts)
    key_grads, value_grads = final_state
    grad_query = query_blocks.reshape(STRETCH, HQ, HD)
    back_order = (jnp.arange(STRETCH, dtype=jnp.int32) - offset[0]) % STRETCH
    return (grad_query, key_grads[STRETCH:], value_grads[STRETCH:], key_grads[:STRETCH][back_order], value_grads[:STRETCH][back_order])
```

```python
import functools
import math

import jax
import jax.numpy as jnp
from jax import lax
from jax.experimental import pallas as pl
from jax.experimental.pallas import tpu as pltpu
from jax.sharding import Mesh, PartitionSpec as P

BF, F4 = jnp.bfloat16, jnp.float32
NEG = -1e30
LOG2E = 1.4426950408889634
HD = 128
HEADS = 12
TOK = 128
SUB = 32
HALF = 2048
KB = 512
HPG = 6
ROWS = HPG * TOK
EXP_SCALE = LOG2E / math.sqrt(HD)
SCALE = 1.0 / math.sqrt(HD)
ALL = ("zl", "y", "x", "zh", "core")
COLUMN = ("zh", "core", "zl")


def nt(a, b):
    return lax.dot_general(a, b, (((1,), (1,)), ((), ())), preferred_element_type=F4)


def nn(a, b):
    return lax.dot_general(a, b, (((1,), (0,)), ((), ())), preferred_element_type=F4)


def block_plan(info, half, run):
    off, win, k = info[0] & (HALF - 1), info[1], info[2]
    t0 = run * HALF + k * TOK
    lo, hi = t0 - win + 1, t0 + TOK - 1
    new_base, old_base = HALF * half, HALF * half - 2 * HALF
    nblk = HALF // KB

    first = jnp.maximum(lo, new_base)
    last = jnp.minimum(hi, new_base + HALF - 1)
    new_first = (first - new_base) // KB
    n_new = jnp.where(last >= first, (last - new_base) // KB + 1 - new_first, 0)

    first_o = jnp.maximum(lo, old_base)
    last_o = jnp.minimum(hi, old_base + HALF - 1)
    start = (first_o - old_base + off) & (HALF - 1)
    old_first = start // KB
    n_old = jnp.where(
        last_o >= first_o,
        jnp.minimum((start - old_first * KB + last_o - first_o + KB) // KB, nblk),
        0,
    )

    def block(i):
        is_new = i < n_new
        ya = jnp.where(is_new, new_first + i, (old_first + i - n_new) & (nblk - 1))
        seg = jnp.where(is_new, 0, 1)
        wrap = off - ya * KB
        inside = (wrap > 0) & (wrap < KB)
        old_min = jnp.where(inside, 0, (ya * KB - off) & (HALF - 1)) + old_base
        pmin = jnp.where(is_new, new_base + ya * KB, old_min)
        pmax = jnp.where(is_new | ~inside, pmin + KB - 1, old_base + HALF - 1)
        full = (pmax <= t0) & (pmin > hi - win)

        def bias():
            r = lax.broadcasted_iota(jnp.int32, (KB, TOK), 0)
            res = ya * KB + r
            pos = jnp.where(is_new, new_base + res, ((res - off) & (HALF - 1)) + old_base)
            qp = t0 + lax.broadcasted_iota(jnp.int32, (KB, TOK), 1)
            b = jnp.where((pos <= qp) & (pos > qp - win), 0.0, NEG)
            return jnp.concatenate([b] * HPG, axis=1)

        return seg, ya, full, bias

    return n_new + n_old, block


def load_rows(qd_ref, which, run, hg, dst):
    for j in range(HPG):
        dst[pl.ds(j * TOK, TOK), :] = qd_ref[:, run, which, hg * HPG + j].reshape(TOK, HD)


def stats_kernel(half, first, info, qd_ref, kv_ref, *refs):
    if not first:
        prev, refs = refs[0], refs[1:]
    st_ref, q_s, do_s = refs

    def per_run(run, _):
        n_all, block = block_plan(info, half, run)

        def per_group(hg, _):
            load_rows(qd_ref, 0, run, hg, q_s)
            load_rows(qd_ref, 1, run, hg, do_s)

            def body(i, c):
                seg, yr, full, bias = block(i)
                k = kv_ref[pl.ds(4 * yr, 4), seg, 0].reshape(KB, HD)
                v = kv_ref[pl.ds(4 * yr, 4), seg, 1].reshape(KB, HD)

                def tile(masked, c):
                    m, l, t = c
                    s = nt(k, q_s[...]) * EXP_SCALE
                    if masked:
                        s = s + bias()
                    g3 = nt(v, do_s[...]).reshape(KB // 8, 8, ROWS)
                    s3 = s.reshape(KB // 8, 8, ROWS)
                    m2 = jnp.maximum(m, jnp.max(s3, axis=0))
                    al = jnp.exp2(m - m2)
                    e3 = jnp.exp2(s3 - m2[None])
                    return (m2, l * al + jnp.sum(e3, axis=0), t * al + jnp.sum(e3 * g3, axis=0))

                return lax.cond(full, functools.partial(tile, False), functools.partial(tile, True), c)

            if first:
                init = (jnp.full((8, ROWS), NEG, F4), jnp.zeros((8, ROWS), F4), jnp.zeros((8, ROWS), F4))
            else:
                init = tuple(prev[run, hg, j] for j in range(3))
            out = lax.fori_loop(0, n_all, body, init)
            for j in range(3):
                st_ref[run, hg, j] = out[j]
            return 0

        return lax.fori_loop(0, HEADS // HPG, per_group, 0)

    lax.fori_loop(0, 2, per_run, 0)


def grads_kernel(half, last, info, qd_ref, st_ref, kv_ref, *refs):
    if last:
        prev, refs = refs[0], refs[1:]
    dq_ref, out_ref, q_s, do_s, dqt_s, acc = refs

    def zero(i, _):
        acc[i] = jnp.zeros((2, 2, KB, HD), F4)
        return 0

    lax.fori_loop(0, 4, zero, 0)

    def per_run(run, _):
        n_all, block = block_plan(info, half, run)

        def per_group(hg, _):
            load_rows(qd_ref, 0, run, hg, q_s)
            load_rows(qd_ref, 1, run, hg, do_s)
            m, l, t = (st_ref[run, hg, j] for j in range(3))
            top = jnp.max(m, axis=0, keepdims=True)
            f = jnp.exp2(m - top)
            total = jnp.sum(l * f, axis=0, keepdims=True)
            lse = jnp.broadcast_to(top + jnp.log2(total), (8, ROWS))
            delta = jnp.broadcast_to(jnp.sum(t * f, axis=0, keepdims=True) / total, (8, ROWS))
            if last:
                dqt_s[...] = prev[run, hg]
            else:
                dqt_s[...] = jnp.zeros_like(dqt_s)

            def body(i, _):
                seg, yr, full, bias = block(i)

                def tile(masked):
                    k = kv_ref[pl.ds(4 * yr, 4), seg, 0].reshape(KB, HD)
                    v = kv_ref[pl.ds(4 * yr, 4), seg, 1].reshape(KB, HD)
                    s = nt(k, q_s[...]) * EXP_SCALE
                    if masked:
                        s = s + bias()
                    g3 = nt(v, do_s[...]).reshape(KB // 8, 8, ROWS)
                    p3 = jnp.exp2(s.reshape(KB // 8, 8, ROWS) - lse[None])
                    pb = p3.reshape(KB, ROWS).astype(BF)
                    ds = (p3 * (g3 - delta[None])).reshape(KB, ROWS).astype(BF)
                    acc[yr, seg, 1] += nn(pb, do_s[...])
                    acc[yr, seg, 0] += nn(ds, q_s[...])
                    dqt_s[...] += nn(jnp.transpose(k), ds)

                pl.when(full)(functools.partial(tile, False))
                pl.when(jnp.logical_not(full))(functools.partial(tile, True))
                return 0

            lax.fori_loop(0, n_all, body, 0)
            if last:
                dq = jnp.transpose(dqt_s[...]) * SCALE
                for j in range(HPG):
                    dq_ref[:, run, hg * HPG + j] = (
                        dq[j * TOK : (j + 1) * TOK].astype(dq_ref.dtype).reshape(TOK // SUB, SUB, HD)
                    )
            else:
                dq_ref[run, hg] = dqt_s[...]
            return 0

        return lax.fori_loop(0, HEADS // HPG, per_group, 0)

    lax.fori_loop(0, 2, per_run, 0)
    for yr in range(4):
        for seg in range(2):
            cols = pl.ds(4 * yr, 4)
            out_ref[cols, seg, 0] = (acc[yr, seg, 0] * SCALE).astype(BF).reshape(4, TOK, HD)
            out_ref[cols, seg, 1] = acc[yr, seg, 1].astype(BF).reshape(4, TOK, HD)


VM = pl.BlockSpec(memory_space=pltpu.VMEM)
SM = pl.BlockSpec(memory_space=pltpu.SMEM)
COMMON = (
    pltpu.VMEM((ROWS, HD), BF),
    pltpu.VMEM((ROWS, HD), BF),
)
STAT_SHAPE = (2, HEADS // HPG, 3, 8, ROWS)


def stats_call(half, first, info, qd, kv, prev=None):
    ops = [info, qd, kv] + ([] if first else [prev])
    return pl.pallas_call(
        functools.partial(stats_kernel, half, first),
        out_shape=jax.ShapeDtypeStruct(STAT_SHAPE, F4),
        in_specs=[SM, VM, VM] + ([] if first else [VM]),
        out_specs=VM,
        scratch_shapes=[*COMMON],
        compiler_params=pltpu.CompilerParams(vmem_limit_bytes=48 * 2**20),
        cost_estimate=pl.CostEstimate(flops=2 * 2 * 3072 * 2112 * HD * 2, bytes_accessed=4 << 20, transcendentals=3072 * 2112),
        name="stats%d" % half,
    )(*ops)


def grads_call(half, last, info, qd, stats, kv, prev=None):
    ops = [info, qd, stats, kv] + ([prev] if last else [])
    dq_shape = (
        jax.ShapeDtypeStruct((4, 2, HEADS, SUB, HD), BF)
        if last
        else jax.ShapeDtypeStruct((2, HEADS // HPG, HD, ROWS), F4)
    )
    outs = pl.pallas_call(
        functools.partial(grads_kernel, half, last),
        out_shape=(dq_shape, jax.ShapeDtypeStruct((16, 2, 2, TOK, HD), BF)),
        in_specs=[SM, VM, VM, VM] + ([VM] if last else []),
        out_specs=(VM, VM),
        scratch_shapes=[
            *COMMON,
            pltpu.VMEM((HD, ROWS), F4),
            pltpu.VMEM((4, 2, 2, KB, HD), F4),
        ],
        compiler_params=pltpu.CompilerParams(vmem_limit_bytes=48 * 2**20),
        cost_estimate=pl.CostEstimate(flops=5 * 2 * 3072 * 2112 * HD * 2, bytes_accessed=8 << 20, transcendentals=3072 * 2112),
        name="grads%d" % half,
    )(*ops)
    return outs


def gather_half(new, old):
    block = jnp.broadcast_to(jnp.stack([new, old])[None], (16, 2, 2, TOK, HD))
    return lax.all_to_all(block, ("y", "x"), 0, 0, tiled=True)


def reduce_half(blocks):
    return jnp.sum(lax.all_to_all(blocks, ("y", "x"), 0, 0, tiled=True).astype(F4), axis=0)


def shards(query, key_new, value_new, key_old, value_old, offset, windows, grad_out):
    zl, yy, xx = lax.axis_index("zl"), lax.axis_index("y"), lax.axis_index("x")
    col = 4 * yy + xx
    swap = lambda a: lax.ppermute(a, "zl", [(0, 1), (1, 0)])

    kv = jnp.stack([jnp.stack([key_new, value_new]), jnp.stack([key_old, value_old])])
    kv = jnp.moveaxis(kv, 3, 0)
    mine = jnp.where(zl == 0, kv[0], kv[1])
    theirs = swap(jnp.where(zl == 0, kv[1], kv[0]))
    z0 = jnp.where(zl == 0, mine, theirs)
    z1 = jnp.where(zl == 0, theirs, mine)
    slot = col * TOK + jnp.arange(TOK, dtype=jnp.int32)
    upper = (((slot - offset[0]) & (2 * HALF - 1)) >= HALF)[None, :, None]
    old_hi = jnp.where(upper, z0[1], z1[1])
    old_lo = jnp.where(upper, z1[1], z0[1])

    def rows_of(a):
        return jnp.swapaxes(a, 0, 1).reshape(8, 1, HEADS, SUB, HD)

    qd = jnp.concatenate([rows_of(query), rows_of(grad_out)], axis=1)
    qd = lax.all_to_all(qd, COLUMN, 0, 0, tiled=True).reshape(4, 2, 2, HEADS, SUB, HD)

    kv_hi = gather_half(z1[0], old_hi)
    new_lo, old_lo, kv_hi = lax.optimization_barrier((z0[0], old_lo, kv_hi))
    kv_lo = gather_half(new_lo, old_lo)

    win = jnp.where(zl == 0, windows[0], windows[1])
    zero = jnp.int32(0)
    info = jnp.stack([offset[0], win, col, zero]).astype(jnp.int32)

    stats = stats_call(1, True, info, qd, kv_hi)
    stats = stats_call(0, False, info, qd, kv_lo, stats)
    dq_part, blocks_hi = grads_call(1, False, info, qd, stats, kv_hi)
    sum_hi = reduce_half(blocks_hi)
    dq, blocks_lo = grads_call(0, True, info, qd, stats, kv_lo, dq_part)
    sum_lo = reduce_half(blocks_lo)

    dq = lax.all_to_all(dq.reshape(8, HEADS, SUB, HD), COLUMN, 0, 0, tiled=True)
    grad_query = jnp.swapaxes(dq.reshape(8 * HEADS, SUB, HD), 0, 1).astype(F4)

    r0 = jnp.stack([sum_lo[0], jnp.where(upper, sum_hi[1], sum_lo[1])])
    r1 = jnp.stack([sum_hi[0], jnp.where(upper, sum_lo[1], sum_hi[1])])
    keep = jnp.where(zl == 0, r0, r1)
    got = swap(jnp.where(zl == 0, r1, r0).astype(BF)).astype(F4)
    both = jnp.stack([jnp.where(zl == 0, keep, got), jnp.where(zl == 0, got, keep)], axis=3)
    return (grad_query, both[0, 0], both[0, 1], both[1, 0], both[1, 1])


def solution(mesh):
    fine = Mesh(mesh.devices.reshape(2, 4, 4, 2, 2), ALL)
    tokens = P(ALL, None, None)
    slots = P(("zl", "y", "x"), ("zh", "core"), None)
    return jax.shard_map(
        shards,
        mesh=fine,
        in_specs=(tokens, slots, slots, slots, slots, P(), P(("zh", "core")), tokens),
        out_specs=(tokens, slots, slots, slots, slots),
        check_vma=False,
    )
```

```python
import functools
import math

import jax
import jax.numpy as jnp
from jax import lax
from jax.experimental import pallas as pl
from jax.experimental.pallas import tpu as pltpu
from jax.sharding import Mesh, PartitionSpec as P

BF, F4 = jnp.bfloat16, jnp.float32
NEG = -1e30
LOG2E = 1.4426950408889634
HD = 128
HEADS = 12
TOK = 128
SUB = 32
HALF = 2048
KB = 512
PART = 64
ROWS = HEADS * PART
EXP_SCALE = LOG2E / math.sqrt(HD)
SCALE = 1.0 / math.sqrt(HD)
ALL = ("zl", "yh", "yp", "x", "zh", "core")
COLUMN = ("zh", "yp", "zl")
PLANE = ("yh", "core", "x")


def nt(a, b):
    return lax.dot_general(a, b, (((1,), (1,)), ((), ())), preferred_element_type=F4)


def nn(a, b):
    return lax.dot_general(a, b, (((1,), (0,)), ((), ())), preferred_element_type=F4)


def block_plan(info, half, run):
    off, win, col, core = info[0] & (HALF - 1), info[1], info[2], info[3]
    zl, yp = run // 2, run % 2
    t0 = zl * HALF + (col + 4 * yp) * TOK + core * SUB
    t1 = t0 + 2 * SUB + SUB - 1
    lo = t0 - win + 1
    new_base, old_base = HALF * half, HALF * half - 2 * HALF
    nblk = HALF // KB

    first = jnp.maximum(lo, new_base)
    last = jnp.minimum(t1, new_base + HALF - 1)
    new_first = (first - new_base) // KB
    n_new = jnp.where(last >= first, (last - new_base) // KB + 1 - new_first, 0)

    first_o = jnp.maximum(lo, old_base)
    last_o = jnp.minimum(t1, old_base + HALF - 1)
    start = (first_o - old_base + off) & (HALF - 1)
    old_first = start // KB
    n_old = jnp.where(
        last_o >= first_o,
        jnp.minimum((start - old_first * KB + last_o - first_o + KB) // KB, nblk),
        0,
    )

    def block(i):
        is_new = i < n_new
        ya = jnp.where(is_new, new_first + i, (old_first + i - n_new) & (nblk - 1))
        seg = jnp.where(is_new, 0, 1)
        wrap = off - ya * KB
        inside = (wrap > 0) & (wrap < KB)
        old_min = jnp.where(inside, 0, (ya * KB - off) & (HALF - 1)) + old_base
        pmin = jnp.where(is_new, new_base + ya * KB, old_min)
        pmax = jnp.where(is_new | ~inside, pmin + KB - 1, old_base + HALF - 1)
        full = (pmax <= t0) & (pmin > t1 - win)

        def bias():
            res = ya * KB + lax.broadcasted_iota(jnp.int32, (KB, TOK), 0)
            pos = jnp.where(is_new, new_base + res, ((res - off) & (HALF - 1)) + old_base)
            lane = lax.broadcasted_iota(jnp.int32, (KB, TOK), 1)
            qp = t0 + (lane & (SUB - 1)) + ((lane & SUB) << 1)
            b = jnp.where((pos <= qp) & (pos > qp - win), 0.0, NEG)
            return jnp.concatenate([b] * (ROWS // TOK), axis=1)

        place = ((ya & 1) ^ core, pl.ds(4 * (ya >> 1), 4))
        return seg, ya, place, full, bias

    return n_new + n_old, block


def load_rows(qd_ref, which, run, dst):
    for j in range(HEADS):
        dst[pl.ds(j * PART, PART), :] = qd_ref[:, run % 2, run // 2, which, j].reshape(PART, HD)


def fetch(srcs, kv_s, sem):
    copies = [pltpu.make_async_copy(s, kv_s.at[i], sem.at[i]) for i, s in enumerate(srcs)]
    for c in copies:
        c.start()
    for c in copies:
        c.wait()


def stats_kernel(info, qd_ref, own, other, st_ref, q_s, do_s, kv_s, sem):
    fetch((own, other), kv_s, sem)

    def per_run(run, _):
        load_rows(qd_ref, 0, run, q_s)
        load_rows(qd_ref, 1, run, do_s)
        c = (jnp.full((8, ROWS), NEG, F4), jnp.zeros((8, ROWS), F4), jnp.zeros((8, ROWS), F4))
        for half in (1, 0):
            n_all, block = block_plan(info, half, run)

            def body(i, c, half=half, block=block):
                seg, ya, (rel, cols), full, bias = block(i)
                k = kv_s[rel, cols, half, seg, 0].reshape(KB, HD)
                v = kv_s[rel, cols, half, seg, 1].reshape(KB, HD)

                def tile(masked, c):
                    m, l, t = c
                    s = nt(k, q_s[...]) * EXP_SCALE
                    if masked:
                        s = s + bias()
                    g3 = nt(v, do_s[...]).reshape(KB // 8, 8, ROWS)
                    s3 = s.reshape(KB // 8, 8, ROWS)
                    m2 = jnp.maximum(m, jnp.max(s3, axis=0))
                    al = jnp.exp2(m - m2)
                    e3 = jnp.exp2(s3 - m2[None])
                    return (m2, l * al + jnp.sum(e3, axis=0), t * al + jnp.sum(e3 * g3, axis=0))

                return lax.cond(full, functools.partial(tile, False), functools.partial(tile, True), c)

            c = lax.fori_loop(0, n_all, body, c)
        m, l, t = c
        top = jnp.max(m, axis=0, keepdims=True)
        f = jnp.exp2(m - top)
        total = jnp.sum(l * f, axis=0, keepdims=True)
        st_ref[run, 0] = jnp.broadcast_to(top + jnp.log2(total), (8, ROWS))
        st_ref[run, 1] = jnp.broadcast_to(jnp.sum(t * f, axis=0, keepdims=True) / total, (8, ROWS))
        return 0

    lax.fori_loop(0, 4, per_run, 0)


def grads_kernel(half, last, info, qd_ref, st_ref, own, other, *refs):
    if last:
        prev, refs = refs[0], refs[1:]
    dq_ref, out_ref, q_s, do_s, kv_s, sem, dqt_s, acc = refs
    fetch((own.at[:, half], other.at[:, half]), kv_s, sem)

    def zero(i, _):
        acc[i] = jnp.zeros((2, 2, KB, HD), F4)
        return 0

    lax.fori_loop(0, 4, zero, 0)

    def per_run(run, _):
        n_all, block = block_plan(info, half, run)
        load_rows(qd_ref, 0, run, q_s)
        load_rows(qd_ref, 1, run, do_s)
        lse, delta = st_ref[run, 0], st_ref[run, 1]
        if last:
            dqt_s[...] = prev[run]
        else:
            dqt_s[...] = jnp.zeros_like(dqt_s)

        def body(i, _):
            seg, ya, (rel, cols), full, bias = block(i)

            def tile(masked):
                k = kv_s[rel, cols, seg, 0].reshape(KB, HD)
                v = kv_s[rel, cols, seg, 1].reshape(KB, HD)
                s = nt(k, q_s[...]) * EXP_SCALE
                if masked:
                    s = s + bias()
                g3 = nt(v, do_s[...]).reshape(KB // 8, 8, ROWS)
                p3 = jnp.exp2(s.reshape(KB // 8, 8, ROWS) - lse[None])
                pb = p3.reshape(KB, ROWS).astype(BF)
                ds = (p3 * (g3 - delta[None])).reshape(KB, ROWS).astype(BF)
                acc[ya, seg, 1] += nn(pb, do_s[...])
                acc[ya, seg, 0] += nn(ds, q_s[...])
                dqt_s[...] += nn(jnp.transpose(k), ds)

            pl.when(full)(functools.partial(tile, False))
            pl.when(jnp.logical_not(full))(functools.partial(tile, True))
            return 0

        lax.fori_loop(0, n_all, body, 0)
        if last:
            dq = (jnp.transpose(dqt_s[...]) * SCALE).astype(BF)
            for j in range(HEADS):
                for zh in range(2):
                    rows = dq[j * PART + zh * SUB : j * PART + (zh + 1) * SUB]
                    dq_ref[info[4] ^ (4 * zh + 2 * (run % 2) + run // 2), j] = rows
        else:
            dq_ref[run] = dqt_s[...]
        return 0

    lax.fori_loop(0, 4, per_run, 0)
    for ya in range(4):
        for seg in range(2):
            cols = pl.ds(4 * ya, 4)
            out_ref[cols, seg, 0] = (acc[ya, seg, 0] * SCALE).astype(BF).reshape(4, TOK, HD)
            out_ref[cols, seg, 1] = acc[ya, seg, 1].astype(BF).reshape(4, TOK, HD)


VM = pl.BlockSpec(memory_space=pltpu.VMEM)
SM = pl.BlockSpec(memory_space=pltpu.SMEM)
ANY = pl.BlockSpec(memory_space=pl.ANY)
ROW_SCRATCH = (pltpu.VMEM((ROWS, HD), BF), pltpu.VMEM((ROWS, HD), BF))
PAIRS = 3072 * 3300


def stats_call(info, qd, own, other):
    return pl.pallas_call(
        stats_kernel,
        out_shape=jax.ShapeDtypeStruct((4, 2, 8, ROWS), F4),
        in_specs=[SM, VM, ANY, ANY],
        out_specs=VM,
        scratch_shapes=[
            *ROW_SCRATCH,
            pltpu.VMEM((2, 8, 2, 2, 2, TOK, HD), BF),
            pltpu.SemaphoreType.DMA((2,)),
        ],
        compiler_params=pltpu.CompilerParams(vmem_limit_bytes=26 * 2**20),
        cost_estimate=pl.CostEstimate(flops=8 * PAIRS * HD, bytes_accessed=4 << 20, transcendentals=PAIRS),
        name="stats",
    )(info, qd, own, other)


def grads_call(half, last, info, qd, stats, own, other, prev=None):
    dq_shape = (
        jax.ShapeDtypeStruct((8, HEADS, SUB, HD), BF)
        if last
        else jax.ShapeDtypeStruct((4, HD, ROWS), F4)
    )
    return pl.pallas_call(
        functools.partial(grads_kernel, half, last),
        out_shape=(dq_shape, jax.ShapeDtypeStruct((16, 2, 2, TOK, HD), BF)),
        in_specs=[SM, VM, VM, ANY, ANY] + ([VM] if last else []),
        out_specs=(VM, VM),
        scratch_shapes=[
            *ROW_SCRATCH,
            pltpu.VMEM((2, 8, 2, 2, TOK, HD), BF),
            pltpu.SemaphoreType.DMA((2,)),
            pltpu.VMEM((HD, ROWS), F4),
            pltpu.VMEM((4, 2, 2, KB, HD), F4),
        ],
        compiler_params=pltpu.CompilerParams(vmem_limit_bytes=32 * 2**20),
        cost_estimate=pl.CostEstimate(flops=10 * PAIRS * HD, bytes_accessed=8 << 20, transcendentals=PAIRS // 2),
        name="grads%d" % half,
    )(*([info, qd, stats, own, other] + ([prev] if last else [])))


def place_kernel(info, *refs):
    *pieces, out_ref = refs
    for d, piece in enumerate(pieces):
        out_ref[info[4] ^ d] = piece[...].astype(F4)


def place_call(info, pieces):
    out = pl.pallas_call(
        place_kernel,
        out_shape=jax.ShapeDtypeStruct((8, HEADS, SUB, HD), F4),
        in_specs=[SM] + [VM] * 8,
        out_specs=VM,
        compiler_params=pltpu.CompilerParams(vmem_limit_bytes=8 * 2**20),
        name="place",
    )(info, *pieces)
    return out.reshape(8 * HEADS, SUB, HD)


def across(block, same_z):
    pairs = []
    for z in range(2):
        for p in range(2):
            for c in range(2):
                to = z if same_z else 1 - z
                pairs.append((4 * z + 2 * p + c, 4 * to + 2 * c + p))
    return lax.ppermute(block, ("zl", "yp", "core"), pairs)


def shift_x(block, by):
    return lax.ppermute(block, "x", [((i + by) % 4, i) for i in range(4)])


def spread_column(blocks):
    got = [blocks[0]]
    for d in range(1, 8):
        flip = (d & 1) << 2 | d & 2 | d >> 2
        got.append(lax.ppermute(blocks[d], ("zl", "yp", "zh"), [(i, i ^ flip) for i in range(8)]))
    return got


def reduce_half(blocks):
    return jnp.sum(lax.all_to_all(blocks, PLANE, 0, 0, tiled=True).astype(F4), axis=0)


def shards(query, key_new, value_new, key_old, value_old, offset, windows, grad_out):
    zl, yh, yp, xx, core = (lax.axis_index(a) for a in ("zl", "yh", "yp", "x", "core"))

    wins = lax.ppermute(windows, ("yp", "core"), [(0, 0), (1, 2), (2, 1), (3, 3)])
    win = jnp.where(zl == 0, wins[0], wins[1])

    def rows_of(a):
        return jnp.swapaxes(a, 0, 1).reshape(8, 1, HEADS, SUB, HD)

    qd = jnp.concatenate([rows_of(query), rows_of(grad_out)], axis=1)
    qd = lax.all_to_all(qd, COLUMN, 0, 0, tiled=True).reshape(2, 2, 2, 2, HEADS, SUB, HD)

    kv = jnp.stack([jnp.stack([key_new, value_new]), jnp.stack([key_old, value_old])])
    kv = jnp.moveaxis(kv, 3, 0)
    same = across(jnp.where(zl == 0, kv[0], kv[1]), True)
    other = across(jnp.where(zl == 0, kv[1], kv[0]), False)
    same, other, win = lax.optimization_barrier((same, other, win))
    z0 = jnp.where(zl == 0, same, other)
    z1 = jnp.where(zl == 0, other, same)
    slot = (8 * yh + 4 * core + xx) * TOK + jnp.arange(TOK, dtype=jnp.int32)
    upper = (((slot - offset[0]) & (2 * HALF - 1)) >= HALF)[None, :, None]
    old_hi = jnp.where(upper, z0[1], z1[1])
    old_lo = jnp.where(upper, z1[1], z0[1])
    block = jnp.stack([jnp.stack([z0[0], old_lo]), jnp.stack([z1[0], old_hi])])
    far = lax.ppermute(block, "yh", [(0, 1), (1, 0)])
    pair = jnp.stack([jnp.where(yh == 0, block, far), jnp.where(yh == 0, far, block)])
    parts = jnp.stack([pair] + [shift_x(pair, d) for d in (1, 2, 3)])
    own = jnp.stack([lax.dynamic_index_in_dim(parts, (j - xx) & 3, 0, keepdims=False) for j in range(4)], axis=1)
    own = own.reshape(8, *block.shape)
    own, qd = lax.optimization_barrier((own, qd))
    other = lax.ppermute(own, "core", [(0, 1), (1, 0)])

    rank = 4 * lax.axis_index("zh") + 2 * yp + zl
    info = jnp.stack([offset[0], win, 8 * yh + xx, core, rank]).astype(jnp.int32)

    stats = stats_call(info, qd, own, other)
    dq_part, blocks_hi = grads_call(1, False, info, qd, stats, own, other)
    sum_hi = reduce_half(blocks_hi)
    dq, blocks_lo = grads_call(0, True, info, qd, stats, own, other, dq_part)
    dq, sum_hi = lax.optimization_barrier((dq, sum_hi))
    sum_lo = reduce_half(blocks_lo)

    got = spread_column(dq)
    *ready, sum_lo = lax.optimization_barrier((*got[:6], sum_lo))
    grad_query = jnp.swapaxes(place_call(info, [*ready, *got[6:]]), 0, 1)

    r0 = jnp.stack([sum_lo[0], jnp.where(upper, sum_hi[1], sum_lo[1])]).astype(BF)
    r1 = jnp.stack([sum_hi[0], jnp.where(upper, sum_lo[1], sum_hi[1])]).astype(BF)
    same = across(jnp.where(zl == 0, r0, r1), True).astype(F4)
    other = across(jnp.where(zl == 0, r1, r0), False).astype(F4)
    both = jnp.stack([jnp.where(zl == 0, same, other), jnp.where(zl == 0, other, same)], axis=3)
    return (grad_query, both[0, 0], both[0, 1], both[1, 0], both[1, 1])


def solution(mesh):
    fine = Mesh(mesh.devices.reshape(2, 2, 2, 4, 2, 2), ALL)
    tokens = P(ALL, None, None)
    slots = P(("zl", "yh", "yp", "x"), ("zh", "core"), None)
    return jax.shard_map(
        shards,
        mesh=fine,
        in_specs=(tokens, slots, slots, slots, slots, P(), P(("zh", "core")), tokens),
        out_specs=(tokens, slots, slots, slots, slots),
        check_vma=False,
    )
```

```python
import functools
import math

import jax
import jax.numpy as jnp
from jax import lax
from jax.experimental import pallas as pl
from jax.experimental.pallas import tpu as pltpu
from jax.sharding import Mesh, PartitionSpec as P

BF, F4 = jnp.bfloat16, jnp.float32
NEG = -1e30
LOG2E = 1.4426950408889634
HD = 128
HEADS = 12
TOK = 128
SUB = 32
HALF = 2048
KB = 512
PART = 64
ROWS = HEADS * PART
EXP_SCALE = LOG2E / math.sqrt(HD)
SCALE = 1.0 / math.sqrt(HD)
ALL = ("zl", "yh", "yp", "x", "zh", "core")
COLUMN = ("zh", "yp", "zl")
PLANE = ("yh", "core", "x")


def nt(a, b):
    return lax.dot_general(a, b, (((1,), (1,)), ((), ())), preferred_element_type=F4)


def nn(a, b):
    return lax.dot_general(a, b, (((1,), (0,)), ((), ())), preferred_element_type=F4)


def block_plan(info, half, run):
    off, win, col, core = info[0] & (HALF - 1), info[1], info[2], info[3]
    zl, yp = run // 2, run % 2
    t0 = zl * HALF + (col + 4 * yp) * TOK + core * SUB
    t1 = t0 + 2 * SUB + SUB - 1
    lo = t0 - win + 1
    new_base, old_base = HALF * half, HALF * half - 2 * HALF
    nblk = HALF // KB

    first = jnp.maximum(lo, new_base)
    last = jnp.minimum(t1, new_base + HALF - 1)
    new_first = (first - new_base) // KB
    n_new = jnp.where(last >= first, (last - new_base) // KB + 1 - new_first, 0)

    first_o = jnp.maximum(lo, old_base)
    last_o = jnp.minimum(t1, old_base + HALF - 1)
    start = (first_o - old_base + off) & (HALF - 1)
    old_first = start // KB
    n_old = jnp.where(
        last_o >= first_o,
        jnp.minimum((start - old_first * KB + last_o - first_o + KB) // KB, nblk),
        0,
    )

    def block(i):
        is_new = i < n_new
        ya = jnp.where(is_new, new_first + i, (old_first + i - n_new) & (nblk - 1))
        seg = jnp.where(is_new, 0, 1)
        wrap = off - ya * KB
        inside = (wrap > 0) & (wrap < KB)
        old_min = jnp.where(inside, 0, (ya * KB - off) & (HALF - 1)) + old_base
        pmin = jnp.where(is_new, new_base + ya * KB, old_min)
        pmax = jnp.where(is_new | ~inside, pmin + KB - 1, old_base + HALF - 1)
        full = (pmax <= t0) & (pmin > t1 - win)

        def bias():
            res = ya * KB + lax.broadcasted_iota(jnp.int32, (KB, TOK), 0)
            pos = jnp.where(is_new, new_base + res, ((res - off) & (HALF - 1)) + old_base)
            lane = lax.broadcasted_iota(jnp.int32, (KB, TOK), 1)
            qp = t0 + (lane & (SUB - 1)) + ((lane & SUB) << 1)
            b = jnp.where((pos <= qp) & (pos > qp - win), 0.0, NEG)
            return jnp.concatenate([b] * (ROWS // TOK), axis=1)

        place = ((ya & 1) ^ core, pl.ds(4 * (ya >> 1), 4))
        return seg, ya, place, full, bias

    return n_new + n_old, block


def load_rows(qd_ref, which, run, dst):
    for j in range(HEADS):
        dst[pl.ds(j * PART, PART), :] = qd_ref[:, run % 2, run // 2, which, j].reshape(PART, HD)


def fetch(srcs, kv_s, sem):
    copies = [pltpu.make_async_copy(s, kv_s.at[i], sem.at[i]) for i, s in enumerate(srcs)]
    for c in copies:
        c.start()
    for c in copies:
        c.wait()


def stats_kernel(info, qd_ref, own, other, st_ref, q_s, do_s, kv_s, sem):
    fetch((own, other), kv_s, sem)

    def per_run(run, _):
        load_rows(qd_ref, 0, run, q_s)
        load_rows(qd_ref, 1, run, do_s)
        c = (jnp.full((8, ROWS), NEG, F4), jnp.zeros((8, ROWS), F4), jnp.zeros((8, ROWS), F4))
        for half in (1, 0):
            n_all, block = block_plan(info, half, run)

            def body(i, c, half=half, block=block):
                seg, ya, (rel, cols), full, bias = block(i)
                k = kv_s[rel, cols, half, seg, 0].reshape(KB, HD)
                v = kv_s[rel, cols, half, seg, 1].reshape(KB, HD)

                def tile(masked, c):
                    m, l, t = c
                    s = nt(k, q_s[...]) * EXP_SCALE
                    if masked:
                        s = s + bias()
                    g3 = nt(v, do_s[...]).reshape(KB // 8, 8, ROWS)
                    s3 = s.reshape(KB // 8, 8, ROWS)
                    m2 = jnp.maximum(m, jnp.max(s3, axis=0))
                    al = jnp.exp2(m - m2)
                    e3 = jnp.exp2(s3 - m2[None])
                    return (m2, l * al + jnp.sum(e3, axis=0), t * al + jnp.sum(e3 * g3, axis=0))

                return lax.cond(full, functools.partial(tile, False), functools.partial(tile, True), c)

            c = lax.fori_loop(0, n_all, body, c)
        m, l, t = c
        top = jnp.max(m, axis=0, keepdims=True)
        f = jnp.exp2(m - top)
        total = jnp.sum(l * f, axis=0, keepdims=True)
        st_ref[run, 0] = jnp.broadcast_to(top + jnp.log2(total), (8, ROWS))
        st_ref[run, 1] = jnp.broadcast_to(jnp.sum(t * f, axis=0, keepdims=True) / total, (8, ROWS))
        return 0

    lax.fori_loop(0, 4, per_run, 0)


def grads_kernel(half, last, info, qd_ref, st_ref, own, other, *refs):
    if last:
        prev, refs = refs[0], refs[1:]
    dq_ref, *out_refs, q_s, do_s, kv_s, sem, dqt_s, acc = refs
    fetch((own.at[:, half], other.at[:, half]), kv_s, sem)

    def zero(i, _):
        acc[i] = jnp.zeros((2, 2, KB, HD), F4)
        return 0

    lax.fori_loop(0, 4, zero, 0)

    def per_run(run, _):
        n_all, block = block_plan(info, half, run)
        load_rows(qd_ref, 0, run, q_s)
        load_rows(qd_ref, 1, run, do_s)
        lse, delta = st_ref[run, 0], st_ref[run, 1]
        if last:
            dqt_s[...] = prev[run]
        else:
            dqt_s[...] = jnp.zeros_like(dqt_s)

        def body(i, _):
            seg, ya, (rel, cols), full, bias = block(i)

            def tile(masked):
                k = kv_s[rel, cols, seg, 0].reshape(KB, HD)
                v = kv_s[rel, cols, seg, 1].reshape(KB, HD)
                s = nt(k, q_s[...]) * EXP_SCALE
                if masked:
                    s = s + bias()
                g3 = nt(v, do_s[...]).reshape(KB // 8, 8, ROWS)
                p3 = jnp.exp2(s.reshape(KB // 8, 8, ROWS) - lse[None])
                pb = p3.reshape(KB, ROWS).astype(BF)
                ds = (p3 * (g3 - delta[None])).reshape(KB, ROWS).astype(BF)
                acc[ya, seg, 1] += nn(pb, do_s[...])
                acc[ya, seg, 0] += nn(ds, q_s[...])
                dqt_s[...] += nn(jnp.transpose(k), ds)

            pl.when(full)(functools.partial(tile, False))
            pl.when(jnp.logical_not(full))(functools.partial(tile, True))
            return 0

        lax.fori_loop(0, n_all, body, 0)
        if last:
            dq = (jnp.transpose(dqt_s[...]) * SCALE).astype(BF)
            for j in range(HEADS):
                for zh in range(2):
                    rows = dq[j * PART + zh * SUB : j * PART + (zh + 1) * SUB]
                    dq_ref[info[4] ^ (4 * zh + 2 * (run % 2) + run // 2), j] = rows
        else:
            dq_ref[run] = dqt_s[...]
        return 0

    lax.fori_loop(0, 4, per_run, 0)
    for i in range(4):
        for seg in range(2):
            if last:
                out_ref, cols = out_refs[i % 2], pl.ds(4 * (i // 2), 4)
                ya = 2 * (i // 2) + ((i % 2) ^ info[3])
            else:
                out_ref, cols, ya = out_refs[0], pl.ds(4 * i, 4), i
            keys, values = acc[ya, seg, 0] * SCALE, acc[ya, seg, 1]
            out_ref[cols, seg, 0] = keys.astype(out_ref.dtype).reshape(4, TOK, HD)
            out_ref[cols, seg, 1] = values.astype(out_ref.dtype).reshape(4, TOK, HD)


VM = pl.BlockSpec(memory_space=pltpu.VMEM)
SM = pl.BlockSpec(memory_space=pltpu.SMEM)
ANY = pl.BlockSpec(memory_space=pl.ANY)
ROW_SCRATCH = (pltpu.VMEM((ROWS, HD), BF), pltpu.VMEM((ROWS, HD), BF))
PAIRS = 3072 * 3300


def stats_call(info, qd, own, other):
    return pl.pallas_call(
        stats_kernel,
        out_shape=jax.ShapeDtypeStruct((4, 2, 8, ROWS), F4),
        in_specs=[SM, VM, ANY, ANY],
        out_specs=VM,
        scratch_shapes=[
            *ROW_SCRATCH,
            pltpu.VMEM((2, 8, 2, 2, 2, TOK, HD), BF),
            pltpu.SemaphoreType.DMA((2,)),
        ],
        compiler_params=pltpu.CompilerParams(vmem_limit_bytes=26 * 2**20),
        cost_estimate=pl.CostEstimate(flops=8 * PAIRS * HD, bytes_accessed=4 << 20, transcendentals=PAIRS),
        name="stats",
    )(info, qd, own, other)


def grads_call(half, last, info, qd, stats, own, other, prev=None):
    dq_shape = (
        jax.ShapeDtypeStruct((8, HEADS, SUB, HD), BF)
        if last
        else jax.ShapeDtypeStruct((4, HD, ROWS), F4)
    )
    sums = (
        [jax.ShapeDtypeStruct((8, 2, 2, TOK, HD), F4)] * 2
        if last
        else [jax.ShapeDtypeStruct((16, 2, 2, TOK, HD), BF)]
    )
    return pl.pallas_call(
        functools.partial(grads_kernel, half, last),
        out_shape=(dq_shape, *sums),
        in_specs=[SM, VM, VM, ANY, ANY] + ([VM] if last else []),
        out_specs=(VM,) * (1 + len(sums)),
        scratch_shapes=[
            *ROW_SCRATCH,
            pltpu.VMEM((2, 8, 2, 2, TOK, HD), BF),
            pltpu.SemaphoreType.DMA((2,)),
            pltpu.VMEM((HD, ROWS), F4),
            pltpu.VMEM((4, 2, 2, KB, HD), F4),
        ],
        compiler_params=pltpu.CompilerParams(vmem_limit_bytes=32 * 2**20),
        cost_estimate=pl.CostEstimate(flops=10 * PAIRS * HD, bytes_accessed=8 << 20, transcendentals=PAIRS // 2),
        name="grads%d" % half,
    )(*([info, qd, stats, own, other] + ([prev] if last else [])))


def place_kernel(info, *refs):
    *pieces, out_ref = refs
    for d, piece in enumerate(pieces):
        out_ref[info[4] ^ d] = piece[...].astype(F4)


def place_call(info, pieces):
    out = pl.pallas_call(
        place_kernel,
        out_shape=jax.ShapeDtypeStruct((8, HEADS, SUB, HD), F4),
        in_specs=[SM] + [VM] * 8,
        out_specs=VM,
        compiler_params=pltpu.CompilerParams(vmem_limit_bytes=8 * 2**20),
        name="place",
    )(info, *pieces)
    return out.reshape(8 * HEADS, SUB, HD)


def across(block, same_z):
    pairs = []
    for z in range(2):
        for p in range(2):
            for c in range(2):
                to = z if same_z else 1 - z
                pairs.append((4 * z + 2 * p + c, 4 * to + 2 * c + p))
    return lax.ppermute(block, ("zl", "yp", "core"), pairs)


def shift_x(block, by):
    return lax.ppermute(block, "x", [((i + by) % 4, i) for i in range(4)])


def spread_column(blocks):
    def swap(d, block):
        flip = (d & 1) << 2 | d & 2 | d >> 2
        return lax.ppermute(block, ("zl", "yp", "zh"), [(i, i ^ flip) for i in range(8)])

    return [blocks[0]] + [swap(d, blocks[d]) for d in range(1, 8)]


def reduce_half(blocks):
    return jnp.sum(lax.all_to_all(blocks, PLANE, 0, 0, tiled=True).astype(F4), axis=0)


def shards(query, key_new, value_new, key_old, value_old, offset, windows, grad_out):
    zl, yh, yp, xx, core = (lax.axis_index(a) for a in ("zl", "yh", "yp", "x", "core"))

    wins = lax.ppermute(windows, ("yp", "core"), [(0, 0), (1, 2), (2, 1), (3, 3)])
    win = jnp.where(zl == 0, wins[0], wins[1])

    def rows_of(a):
        return jnp.swapaxes(a, 0, 1).reshape(8, 1, HEADS, SUB, HD)

    qd = jnp.concatenate([rows_of(query), rows_of(grad_out)], axis=1)
    qd = lax.all_to_all(qd, COLUMN, 0, 0, tiled=True).reshape(2, 2, 2, 2, HEADS, SUB, HD)

    kv = jnp.stack([jnp.stack([key_new, value_new]), jnp.stack([key_old, value_old])])
    kv = jnp.moveaxis(kv, 3, 0)
    same = across(jnp.where(zl == 0, kv[0], kv[1]), True)
    other = across(jnp.where(zl == 0, kv[1], kv[0]), False)
    same, other, win = lax.optimization_barrier((same, other, win))
    z0 = jnp.where(zl == 0, same, other)
    z1 = jnp.where(zl == 0, other, same)
    slot = (8 * yh + 4 * core + xx) * TOK + jnp.arange(TOK, dtype=jnp.int32)
    upper = (((slot - offset[0]) & (2 * HALF - 1)) >= HALF)[None, :, None]
    old_hi = jnp.where(upper, z0[1], z1[1])
    old_lo = jnp.where(upper, z1[1], z0[1])
    block = jnp.stack([jnp.stack([z0[0], old_lo]), jnp.stack([z1[0], old_hi])])
    far = lax.ppermute(block, "yh", [(0, 1), (1, 0)])
    pair = jnp.stack([jnp.where(yh == 0, block, far), jnp.where(yh == 0, far, block)])
    parts = jnp.stack([pair] + [shift_x(pair, d) for d in (1, 2, 3)])
    own = jnp.stack([lax.dynamic_index_in_dim(parts, (j - xx) & 3, 0, keepdims=False) for j in range(4)], axis=1)
    own = own.reshape(8, *block.shape)
    own, qd = lax.optimization_barrier((own, qd))
    other = lax.ppermute(own, "core", [(0, 1), (1, 0)])

    rank = 4 * lax.axis_index("zh") + 2 * yp + zl
    info = jnp.stack([offset[0], win, 8 * yh + xx, core, rank]).astype(jnp.int32)

    stats = stats_call(info, qd, own, other)
    dq_part, blocks_hi = grads_call(1, False, info, qd, stats, own, other)
    sum_hi = reduce_half(blocks_hi)
    dq, share, others = grads_call(0, True, info, qd, stats, own, other, dq_part)
    others, sum_hi = lax.optimization_barrier((others, sum_hi))
    share = (share + lax.ppermute(others, "core", [(0, 1), (1, 0)])).astype(BF)
    got = spread_column(dq)
    *some, share = lax.optimization_barrier((*got[1:5], share))
    got[1:5] = some
    sum_lo = jnp.sum(lax.all_to_all(share, ("yh", "x"), 0, 0, tiled=True).astype(F4), axis=0)

    grad_query = jnp.swapaxes(place_call(info, got), 0, 1)

    r0 = jnp.stack([sum_lo[0], jnp.where(upper, sum_hi[1], sum_lo[1])]).astype(BF)
    r1 = jnp.stack([sum_hi[0], jnp.where(upper, sum_lo[1], sum_hi[1])]).astype(BF)
    same = across(jnp.where(zl == 0, r0, r1), True).astype(F4)
    other = across(jnp.where(zl == 0, r1, r0), False).astype(F4)
    both = jnp.stack([jnp.where(zl == 0, same, other), jnp.where(zl == 0, other, same)], axis=3)
    return (grad_query, both[0, 0], both[0, 1], both[1, 0], both[1, 1])


def solution(mesh):
    fine = Mesh(mesh.devices.reshape(2, 2, 2, 4, 2, 2), ALL)
    tokens = P(ALL, None, None)
    slots = P(("zl", "yh", "yp", "x"), ("zh", "core"), None)
    return jax.shard_map(
        shards,
        mesh=fine,
        in_specs=(tokens, slots, slots, slots, slots, P(), P(("zh", "core")), tokens),
        out_specs=(tokens, slots, slots, slots, slots),
        check_vma=False,
    )
```

```python
import functools
import math

import jax
import jax.numpy as jnp
from jax import lax
from jax.experimental import pallas as pl
from jax.experimental.pallas import tpu as pltpu
from jax.sharding import Mesh, PartitionSpec as P

BF, F4 = jnp.bfloat16, jnp.float32
NEG = -1e30
LOG2E = 1.4426950408889634
HD = 128
HEADS = 12
TOK = 128
SUB = 32
HALF = 2048
KB = 512
PART = 64
ROWS = HEADS * PART
EXP_SCALE = LOG2E / math.sqrt(HD)
SCALE = 1.0 / math.sqrt(HD)
ALL = ("zl", "yh", "yp", "x", "zh", "core")
COLUMN = ("zh", "yp", "zl")
PLANE = ("yh", "core", "x")


def nt(a, b):
    return lax.dot_general(a, b, (((1,), (1,)), ((), ())), preferred_element_type=F4)


def nn(a, b):
    return lax.dot_general(a, b, (((1,), (0,)), ((), ())), preferred_element_type=F4)


def block_plan(info, half, run):
    off, win, col, core = info[0] & (HALF - 1), info[1], info[2], info[3]
    zl, yp = run // 2, run % 2
    t0 = zl * HALF + (col + 4 * yp) * TOK + core * SUB
    t1 = t0 + 2 * SUB + SUB - 1
    lo = t0 - win + 1
    new_base, old_base = HALF * half, HALF * half - 2 * HALF
    nblk = HALF // KB

    first = jnp.maximum(lo, new_base)
    last = jnp.minimum(t1, new_base + HALF - 1)
    new_first = (first - new_base) // KB
    n_new = jnp.where(last >= first, (last - new_base) // KB + 1 - new_first, 0)

    first_o = jnp.maximum(lo, old_base)
    last_o = jnp.minimum(t1, old_base + HALF - 1)
    start = (first_o - old_base + off) & (HALF - 1)
    old_first = start // KB
    n_old = jnp.where(
        last_o >= first_o,
        jnp.minimum((start - old_first * KB + last_o - first_o + KB) // KB, nblk),
        0,
    )

    def block(i):
        is_new = i < n_new
        ya = jnp.where(is_new, new_first + i, (old_first + i - n_new) & (nblk - 1))
        seg = jnp.where(is_new, 0, 1)
        wrap = off - ya * KB
        inside = (wrap > 0) & (wrap < KB)
        old_min = jnp.where(inside, 0, (ya * KB - off) & (HALF - 1)) + old_base
        pmin = jnp.where(is_new, new_base + ya * KB, old_min)
        pmax = jnp.where(is_new | ~inside, pmin + KB - 1, old_base + HALF - 1)
        full = (pmax <= t0) & (pmin > t1 - win)

        def bias():
            res = ya * KB + lax.broadcasted_iota(jnp.int32, (KB, TOK), 0)
            pos = jnp.where(is_new, new_base + res, ((res - off) & (HALF - 1)) + old_base)
            lane = lax.broadcasted_iota(jnp.int32, (KB, TOK), 1)
            qp = t0 + (lane & (SUB - 1)) + ((lane & SUB) << 1)
            b = jnp.where((pos <= qp) & (pos > qp - win), 0.0, NEG)
            return jnp.concatenate([b] * (ROWS // TOK), axis=1)

        place = ((ya & 1) ^ core, pl.ds(4 * (ya >> 1), 4))
        return seg, ya, place, full, bias

    return n_new + n_old, block


def load_rows(qd_ref, which, run, dst):
    for j in range(HEADS):
        dst[pl.ds(j * PART, PART), :] = qd_ref[:, run % 2, run // 2, which, j].reshape(PART, HD)


def fetch(srcs, kv_s, sem):
    copies = [pltpu.make_async_copy(s, kv_s.at[i], sem.at[i]) for i, s in enumerate(srcs)]
    for c in copies:
        c.start()
    for c in copies:
        c.wait()


def stats_kernel(info, qd_ref, own, other, st_ref, q_s, do_s, kv_s, sem):
    fetch((own, other), kv_s, sem)

    def per_run(run, _):
        load_rows(qd_ref, 0, run, q_s)
        load_rows(qd_ref, 1, run, do_s)
        c = (jnp.full((8, ROWS), NEG, F4), jnp.zeros((8, ROWS), F4), jnp.zeros((8, ROWS), F4))
        for half in (1, 0):
            n_all, block = block_plan(info, half, run)

            def body(i, c, half=half, block=block):
                seg, ya, (rel, cols), full, bias = block(i)
                k = kv_s[rel, cols, half, seg, 0].reshape(KB, HD)
                v = kv_s[rel, cols, half, seg, 1].reshape(KB, HD)

                def tile(masked, c):
                    m, l, t = c
                    s = nt(k, q_s[...]) * EXP_SCALE
                    if masked:
                        s = s + bias()
                    g3 = nt(v, do_s[...]).reshape(KB // 8, 8, ROWS)
                    s3 = s.reshape(KB // 8, 8, ROWS)
                    m2 = jnp.maximum(m, jnp.max(s3, axis=0))
                    al = jnp.exp2(m - m2)
                    e3 = jnp.exp2(s3 - m2[None])
                    return (m2, l * al + jnp.sum(e3, axis=0), t * al + jnp.sum(e3 * g3, axis=0))

                return lax.cond(full, functools.partial(tile, False), functools.partial(tile, True), c)

            c = lax.fori_loop(0, n_all, body, c)
        m, l, t = c
        top = jnp.max(m, axis=0, keepdims=True)
        f = jnp.exp2(m - top)
        total = jnp.sum(l * f, axis=0, keepdims=True)
        st_ref[run, 0] = jnp.broadcast_to(top + jnp.log2(total), (8, ROWS))
        st_ref[run, 1] = jnp.broadcast_to(jnp.sum(t * f, axis=0, keepdims=True) / total, (8, ROWS))
        return 0

    lax.fori_loop(0, 4, per_run, 0)


def grads_kernel(half, last, info, qd_ref, st_ref, own, other, *refs):
    if last:
        prev, refs = refs[0], refs[1:]
    dq_ref, *out_refs, q_s, do_s, kv_s, sem, dqt_s, acc = refs
    fetch((own.at[:, half], other.at[:, half]), kv_s, sem)

    def zero(i, _):
        acc[i] = jnp.zeros((2, 2, KB, HD), F4)
        return 0

    lax.fori_loop(0, 4, zero, 0)

    def per_run(run, _):
        n_all, block = block_plan(info, half, run)
        load_rows(qd_ref, 0, run, q_s)
        load_rows(qd_ref, 1, run, do_s)
        lse, delta = st_ref[run, 0], st_ref[run, 1]
        if last:
            dqt_s[...] = prev[run]
        else:
            dqt_s[...] = jnp.zeros_like(dqt_s)

        def body(i, _):
            seg, ya, (rel, cols), full, bias = block(i)

            def tile(masked):
                k = kv_s[rel, cols, seg, 0].reshape(KB, HD)
                v = kv_s[rel, cols, seg, 1].reshape(KB, HD)
                s = nt(k, q_s[...]) * EXP_SCALE
                if masked:
                    s = s + bias()
                g3 = nt(v, do_s[...]).reshape(KB // 8, 8, ROWS)
                p3 = jnp.exp2(s.reshape(KB // 8, 8, ROWS) - lse[None])
                pb = p3.reshape(KB, ROWS).astype(BF)
                ds = (p3 * (g3 - delta[None])).reshape(KB, ROWS).astype(BF)
                acc[ya, seg, 1] += nn(pb, do_s[...])
                acc[ya, seg, 0] += nn(ds, q_s[...])
                dqt_s[...] += nn(jnp.transpose(k), ds)

            pl.when(full)(functools.partial(tile, False))
            pl.when(jnp.logical_not(full))(functools.partial(tile, True))
            return 0

        lax.fori_loop(0, n_all, body, 0)
        if last:
            dq = (jnp.transpose(dqt_s[...]) * SCALE).astype(BF)
            for j in range(HEADS):
                for zh in range(2):
                    rows = dq[j * PART + zh * SUB : j * PART + (zh + 1) * SUB]
                    dq_ref[4 * zh + 2 * (run % 2) + run // 2, j] = rows
        else:
            dq_ref[run] = dqt_s[...]
        return 0

    lax.fori_loop(0, 4, per_run, 0)
    for i in range(4):
        for seg in range(2):
            if last:
                out_ref, cols = out_refs[i % 2], pl.ds(4 * (i // 2), 4)
                ya = 2 * (i // 2) + ((i % 2) ^ info[3])
            else:
                out_ref, cols, ya = out_refs[0], pl.ds(4 * i, 4), i
            keys, values = acc[ya, seg, 0] * SCALE, acc[ya, seg, 1]
            out_ref[cols, seg, 0] = keys.astype(out_ref.dtype).reshape(4, TOK, HD)
            out_ref[cols, seg, 1] = values.astype(out_ref.dtype).reshape(4, TOK, HD)


VM = pl.BlockSpec(memory_space=pltpu.VMEM)
SM = pl.BlockSpec(memory_space=pltpu.SMEM)
ANY = pl.BlockSpec(memory_space=pl.ANY)
ROW_SCRATCH = (pltpu.VMEM((ROWS, HD), BF), pltpu.VMEM((ROWS, HD), BF))
PAIRS = 3072 * 3300


def stats_call(info, qd, own, other):
    return pl.pallas_call(
        stats_kernel,
        out_shape=jax.ShapeDtypeStruct((4, 2, 8, ROWS), F4),
        in_specs=[SM, VM, ANY, ANY],
        out_specs=VM,
        scratch_shapes=[
            *ROW_SCRATCH,
            pltpu.VMEM((2, 8, 2, 2, 2, TOK, HD), BF),
            pltpu.SemaphoreType.DMA((2,)),
        ],
        compiler_params=pltpu.CompilerParams(vmem_limit_bytes=26 * 2**20),
        cost_estimate=pl.CostEstimate(flops=8 * PAIRS * HD, bytes_accessed=4 << 20, transcendentals=PAIRS),
        name="stats",
    )(info, qd, own, other)


def grads_call(half, last, info, qd, stats, own, other, prev=None):
    dq_shape = (
        jax.ShapeDtypeStruct((8, HEADS, SUB, HD), BF)
        if last
        else jax.ShapeDtypeStruct((4, HD, ROWS), F4)
    )
    sums = (
        [jax.ShapeDtypeStruct((8, 2, 2, TOK, HD), F4)] * 2
        if last
        else [jax.ShapeDtypeStruct((16, 2, 2, TOK, HD), BF)]
    )
    return pl.pallas_call(
        functools.partial(grads_kernel, half, last),
        out_shape=(dq_shape, *sums),
        in_specs=[SM, VM, VM, ANY, ANY] + ([VM] if last else []),
        out_specs=(VM,) * (1 + len(sums)),
        scratch_shapes=[
            *ROW_SCRATCH,
            pltpu.VMEM((2, 8, 2, 2, TOK, HD), BF),
            pltpu.SemaphoreType.DMA((2,)),
            pltpu.VMEM((HD, ROWS), F4),
            pltpu.VMEM((4, 2, 2, KB, HD), F4),
        ],
        compiler_params=pltpu.CompilerParams(vmem_limit_bytes=32 * 2**20),
        cost_estimate=pl.CostEstimate(flops=10 * PAIRS * HD, bytes_accessed=8 << 20, transcendentals=PAIRS // 2),
        name="grads%d" % half,
    )(*([info, qd, stats, own, other] + ([prev] if last else [])))


def across(block, same_z):
    pairs = []
    for z in range(2):
        for p in range(2):
            for c in range(2):
                to = z if same_z else 1 - z
                pairs.append((4 * z + 2 * p + c, 4 * to + 2 * c + p))
    return lax.ppermute(block, ("zl", "yp", "core"), pairs)


def shift_x(block, by):
    return lax.ppermute(block, "x", [((i + by) % 4, i) for i in range(4)])


def reduce_half(blocks):
    return jnp.sum(lax.all_to_all(blocks, PLANE, 0, 0, tiled=True).astype(F4), axis=0)


def shards(query, key_new, value_new, key_old, value_old, offset, windows, grad_out):
    zl, yh, yp, xx, core = (lax.axis_index(a) for a in ("zl", "yh", "yp", "x", "core"))

    wins = lax.ppermute(windows, ("yp", "core"), [(0, 0), (1, 2), (2, 1), (3, 3)])
    win = jnp.where(zl == 0, wins[0], wins[1])

    def rows_of(a):
        return jnp.swapaxes(a, 0, 1).reshape(8, 1, HEADS, SUB, HD)

    qd = jnp.concatenate([rows_of(query), rows_of(grad_out)], axis=1)
    qd = lax.all_to_all(qd, COLUMN, 0, 0, tiled=True).reshape(2, 2, 2, 2, HEADS, SUB, HD)

    kv = jnp.stack([jnp.stack([key_new, value_new]), jnp.stack([key_old, value_old])])
    kv = jnp.moveaxis(kv, 3, 0)
    same = across(jnp.where(zl == 0, kv[0], kv[1]), True)
    other = across(jnp.where(zl == 0, kv[1], kv[0]), False)
    same, other, win = lax.optimization_barrier((same, other, win))
    z0 = jnp.where(zl == 0, same, other)
    z1 = jnp.where(zl == 0, other, same)
    slot = (8 * yh + 4 * core + xx) * TOK + jnp.arange(TOK, dtype=jnp.int32)
    upper = (((slot - offset[0]) & (2 * HALF - 1)) >= HALF)[None, :, None]
    old_hi = jnp.where(upper, z0[1], z1[1])
    old_lo = jnp.where(upper, z1[1], z0[1])
    block = jnp.stack([jnp.stack([z0[0], old_lo]), jnp.stack([z1[0], old_hi])])
    far = lax.ppermute(block, "yh", [(0, 1), (1, 0)])
    pair = jnp.stack([jnp.where(yh == 0, block, far), jnp.where(yh == 0, far, block)])
    parts = jnp.stack([pair] + [shift_x(pair, d) for d in (1, 2, 3)])
    own = jnp.stack([lax.dynamic_index_in_dim(parts, (j - xx) & 3, 0, keepdims=False) for j in range(4)], axis=1)
    own = own.reshape(8, *block.shape)
    own, qd = lax.optimization_barrier((own, qd))
    other = lax.ppermute(own, "core", [(0, 1), (1, 0)])

    info = jnp.stack([offset[0], win, 8 * yh + xx, core]).astype(jnp.int32)

    stats = stats_call(info, qd, own, other)
    dq_part, blocks_hi = grads_call(1, False, info, qd, stats, own, other)
    sum_hi = reduce_half(blocks_hi)
    dq, share, others = grads_call(0, True, info, qd, stats, own, other, dq_part)
    others, sum_hi = lax.optimization_barrier((others, sum_hi))
    share = (share + lax.ppermute(others, "core", [(0, 1), (1, 0)])).astype(BF)
    dq = lax.all_to_all(dq, COLUMN, 0, 0, tiled=True)
    dq, share = lax.optimization_barrier((dq, share))
    sum_lo = jnp.sum(lax.all_to_all(share, ("yh", "x"), 0, 0, tiled=True).astype(F4), axis=0)

    grad_query = jnp.swapaxes(dq.reshape(8 * HEADS, SUB, HD), 0, 1).astype(F4)

    r0 = jnp.stack([sum_lo[0], jnp.where(upper, sum_hi[1], sum_lo[1])]).astype(BF)
    r1 = jnp.stack([sum_hi[0], jnp.where(upper, sum_lo[1], sum_hi[1])]).astype(BF)
    same = across(jnp.where(zl == 0, r0, r1), True).astype(F4)
    other = across(jnp.where(zl == 0, r1, r0), False).astype(F4)
    both = jnp.stack([jnp.where(zl == 0, same, other), jnp.where(zl == 0, other, same)], axis=3)
    return (grad_query, both[0, 0], both[0, 1], both[1, 0], both[1, 1])


def solution(mesh):
    fine = Mesh(mesh.devices.reshape(2, 2, 2, 4, 2, 2), ALL)
    tokens = P(ALL, None, None)
    slots = P(("zl", "yh", "yp", "x"), ("zh", "core"), None)
    return jax.shard_map(
        shards,
        mesh=fine,
        in_specs=(tokens, slots, slots, slots, slots, P(), P(("zh", "core")), tokens),
        out_specs=(tokens, slots, slots, slots, slots),
        check_vma=False,
    )
```

```python
import functools
import math

import jax
import jax.numpy as jnp
from jax import lax
from jax.experimental import pallas as pl
from jax.experimental.pallas import tpu as pltpu
from jax.sharding import Mesh, PartitionSpec as P

BF, F4 = jnp.bfloat16, jnp.float32
NEG = -1e30
LOG2E = 1.4426950408889634
HD = 128
HEADS = 12
TOK = 128
SUB = 32
HALF = 2048
KB = 512
PART = 64
ROWS = HEADS * PART
EXP_SCALE = LOG2E / math.sqrt(HD)
SCALE = 1.0 / math.sqrt(HD)
ALL = ("zl", "yh", "yp", "x", "zh", "core")
COLUMN = ("zh", "yp", "zl")
PLANE = ("yh", "core", "x")


def nt(a, b):
    return lax.dot_general(a, b, (((1,), (1,)), ((), ())), preferred_element_type=F4)


def nn(a, b):
    return lax.dot_general(a, b, (((1,), (0,)), ((), ())), preferred_element_type=F4)


def block_plan(info, half, run):
    off, win, col, core = info[0] & (HALF - 1), info[1], info[2], info[3]
    zl, yp = run // 2, run % 2
    t0 = zl * HALF + (col + 4 * yp) * TOK + core * SUB
    t1 = t0 + 2 * SUB + SUB - 1
    lo = t0 - win + 1
    new_base, old_base = HALF * half, HALF * half - 2 * HALF
    nblk = HALF // KB

    first = jnp.maximum(lo, new_base)
    last = jnp.minimum(t1, new_base + HALF - 1)
    new_first = (first - new_base) // KB
    n_new = jnp.where(last >= first, (last - new_base) // KB + 1 - new_first, 0)

    first_o = jnp.maximum(lo, old_base)
    last_o = jnp.minimum(t1, old_base + HALF - 1)
    start = (first_o - old_base + off) & (HALF - 1)
    old_first = start // KB
    n_old = jnp.where(
        last_o >= first_o,
        jnp.minimum((start - old_first * KB + last_o - first_o + KB) // KB, nblk),
        0,
    )

    def block(i):
        is_new = i < n_new
        ya = jnp.where(is_new, new_first + i, (old_first + i - n_new) & (nblk - 1))
        seg = jnp.where(is_new, 0, 1)
        wrap = off - ya * KB
        inside = (wrap > 0) & (wrap < KB)
        old_min = jnp.where(inside, 0, (ya * KB - off) & (HALF - 1)) + old_base
        pmin = jnp.where(is_new, new_base + ya * KB, old_min)
        pmax = jnp.where(is_new | ~inside, pmin + KB - 1, old_base + HALF - 1)
        full = (pmax <= t0) & (pmin > t1 - win)

        def bias():
            res = ya * KB + lax.broadcasted_iota(jnp.int32, (KB, TOK), 0)
            pos = jnp.where(is_new, new_base + res, ((res - off) & (HALF - 1)) + old_base)
            lane = lax.broadcasted_iota(jnp.int32, (KB, TOK), 1)
            qp = t0 + (lane & (SUB - 1)) + ((lane & SUB) << 1)
            b = jnp.where((pos <= qp) & (pos > qp - win), 0.0, NEG)
            return jnp.concatenate([b] * (ROWS // TOK), axis=1)

        place = ((ya & 1) ^ core, pl.ds(4 * (ya >> 1), 4))
        return seg, ya, place, full, bias

    return n_new + n_old, block


def load_rows(qd_ref, which, run, dst):
    for j in range(HEADS):
        dst[pl.ds(j * PART, PART), :] = qd_ref[:, run % 2, run // 2, which, j].reshape(PART, HD)


def fetch(srcs, kv_s, sem):
    copies = [pltpu.make_async_copy(s, kv_s.at[i], sem.at[i]) for i, s in enumerate(srcs)]
    for c in copies:
        c.start()
    for c in copies:
        c.wait()


def stats_kernel(info, qd_ref, own, other, st_ref, q_s, do_s, kv_s, sem):
    fetch((own, other), kv_s, sem)

    def per_run(run, _):
        load_rows(qd_ref, 0, run, q_s)
        load_rows(qd_ref, 1, run, do_s)
        c = (jnp.full((8, ROWS), NEG, F4), jnp.zeros((8, ROWS), F4), jnp.zeros((8, ROWS), F4))
        for half in (1, 0):
            n_all, block = block_plan(info, half, run)

            def body(i, c, half=half, block=block):
                seg, ya, (rel, cols), full, bias = block(i)
                k = kv_s[rel, cols, half, seg, 0].reshape(KB, HD)
                v = kv_s[rel, cols, half, seg, 1].reshape(KB, HD)

                def tile(masked, c):
                    m, l, t = c
                    s = nt(k, q_s[...]) * EXP_SCALE
                    if masked:
                        s = s + bias()
                    g3 = nt(v, do_s[...]).reshape(KB // 8, 8, ROWS)
                    s3 = s.reshape(KB // 8, 8, ROWS)
                    m2 = jnp.maximum(m, jnp.max(s3, axis=0))
                    al = jnp.exp2(m - m2)
                    e3 = jnp.exp2(s3 - m2[None])
                    return (m2, l * al + jnp.sum(e3, axis=0), t * al + jnp.sum(e3 * g3, axis=0))

                return lax.cond(full, functools.partial(tile, False), functools.partial(tile, True), c)

            c = lax.fori_loop(0, n_all, body, c)
        m, l, t = c
        top = jnp.max(m, axis=0, keepdims=True)
        f = jnp.exp2(m - top)
        total = jnp.sum(l * f, axis=0, keepdims=True)
        st_ref[run, 0] = jnp.broadcast_to(top + jnp.log2(total), (8, ROWS))
        st_ref[run, 1] = jnp.broadcast_to(jnp.sum(t * f, axis=0, keepdims=True) / total, (8, ROWS))
        return 0

    lax.fori_loop(0, 4, per_run, 0)


def grads_kernel(half, last, info, qd_ref, st_ref, own, other, *refs):
    if last:
        prev, refs = refs[0], refs[1:]
    dq_ref, *out_refs, q_s, do_s, kv_s, sem, dq_s, acc, out_s, out_sem, dq_sem = refs
    if last:
        before = pltpu.make_async_copy(prev, dq_s, dq_sem.at[0])
        before.start()
    fetch((own.at[:, half], other.at[:, half]), kv_s, sem)

    def zero(i, _):
        acc[i] = jnp.zeros((2, 2, KB, HD), F4)
        return 0

    lax.fori_loop(0, 4, zero, 0)
    if last:
        before.wait()

    def per_run(run, _):
        n_all, block = block_plan(info, half, run)
        load_rows(qd_ref, 0, run, q_s)
        load_rows(qd_ref, 1, run, do_s)
        lse, delta = st_ref[run, 0], st_ref[run, 1]
        if not last:
            dq_s[run] = jnp.zeros((HD, ROWS), F4)

        def body(i, _):
            seg, ya, (rel, cols), full, bias = block(i)

            def tile(masked):
                k = kv_s[rel, cols, seg, 0].reshape(KB, HD)
                v = kv_s[rel, cols, seg, 1].reshape(KB, HD)
                s = nt(k, q_s[...]) * EXP_SCALE
                if masked:
                    s = s + bias()
                g3 = nt(v, do_s[...]).reshape(KB // 8, 8, ROWS)
                p3 = jnp.exp2(s.reshape(KB // 8, 8, ROWS) - lse[None])
                pb = p3.reshape(KB, ROWS).astype(BF)
                ds = (p3 * (g3 - delta[None])).reshape(KB, ROWS).astype(BF)
                acc[ya, seg, 1] += nn(pb, do_s[...])
                acc[ya, seg, 0] += nn(ds, q_s[...])
                dq_s[run] += nn(jnp.transpose(k), ds)

            pl.when(full)(functools.partial(tile, False))
            pl.when(jnp.logical_not(full))(functools.partial(tile, True))
            return 0

        lax.fori_loop(0, n_all, body, 0)
        if last:
            dq = (jnp.transpose(dq_s[run]) * SCALE).astype(BF)
            for j in range(HEADS):
                for zh in range(2):
                    rows = dq[j * PART + zh * SUB : j * PART + (zh + 1) * SUB]
                    dq_ref[4 * zh + 2 * (run % 2) + run // 2, j] = rows
        return 0

    lax.fori_loop(0, 4, per_run, 0)
    copies = [] if last else [pltpu.make_async_copy(dq_s, dq_ref, dq_sem.at[0])]
    for c in copies:
        c.start()
    for i in range(4):
        if last:
            out_ref, cols = out_refs[i % 2], pl.ds(4 * (i // 2), 4)
            ya = 2 * (i // 2) + ((i % 2) ^ info[3])
        else:
            out_ref, cols, ya = out_refs[0], pl.ds(4 * i, 4), i
        for seg in range(2):
            keys, values = acc[ya, seg, 0] * SCALE, acc[ya, seg, 1]
            out_s[i, :, seg, 0] = keys.astype(out_s.dtype).reshape(4, TOK, HD)
            out_s[i, :, seg, 1] = values.astype(out_s.dtype).reshape(4, TOK, HD)
        copies.append(pltpu.make_async_copy(out_s.at[i], out_ref.at[cols], out_sem.at[i]))
        copies[-1].start()
    for c in copies:
        c.wait()


VM = pl.BlockSpec(memory_space=pltpu.VMEM)
SM = pl.BlockSpec(memory_space=pltpu.SMEM)
ANY = pl.BlockSpec(memory_space=pl.ANY)
ROW_SCRATCH = (pltpu.VMEM((ROWS, HD), BF), pltpu.VMEM((ROWS, HD), BF))
PAIRS = 3072 * 3300


def stats_call(info, qd, own, other):
    return pl.pallas_call(
        stats_kernel,
        out_shape=jax.ShapeDtypeStruct((4, 2, 8, ROWS), F4),
        in_specs=[SM, VM, ANY, ANY],
        out_specs=VM,
        scratch_shapes=[
            *ROW_SCRATCH,
            pltpu.VMEM((2, 8, 2, 2, 2, TOK, HD), BF),
            pltpu.SemaphoreType.DMA((2,)),
        ],
        compiler_params=pltpu.CompilerParams(vmem_limit_bytes=26 * 2**20),
        cost_estimate=pl.CostEstimate(flops=8 * PAIRS * HD, bytes_accessed=4 << 20, transcendentals=PAIRS),
        name="stats",
    )(info, qd, own, other)


def grads_call(half, last, info, qd, stats, own, other, prev=None):
    dq_shape = (
        jax.ShapeDtypeStruct((8, HEADS, SUB, HD), BF)
        if last
        else jax.ShapeDtypeStruct((4, HD, ROWS), F4)
    )
    sums = (
        [jax.ShapeDtypeStruct((8, 2, 2, TOK, HD), F4)] * 2
        if last
        else [jax.ShapeDtypeStruct((16, 2, 2, TOK, HD), BF)]
    )
    return pl.pallas_call(
        functools.partial(grads_kernel, half, last),
        out_shape=(dq_shape, *sums),
        in_specs=[SM, VM, VM, ANY, ANY] + ([ANY] if last else []),
        out_specs=(VM if last else ANY,) + (ANY,) * len(sums),
        scratch_shapes=[
            *ROW_SCRATCH,
            pltpu.VMEM((2, 8, 2, 2, TOK, HD), BF),
            pltpu.SemaphoreType.DMA((2,)),
            pltpu.VMEM((4, HD, ROWS), F4),
            pltpu.VMEM((4, 2, 2, KB, HD), F4),
            pltpu.VMEM((4, 4, 2, 2, TOK, HD), F4 if last else BF),
            pltpu.SemaphoreType.DMA((4,)),
            pltpu.SemaphoreType.DMA((1,)),
        ],
        compiler_params=pltpu.CompilerParams(vmem_limit_bytes=32 * 2**20),
        cost_estimate=pl.CostEstimate(flops=10 * PAIRS * HD, bytes_accessed=8 << 20, transcendentals=PAIRS // 2),
        name="grads%d" % half,
    )(*([info, qd, stats, own, other] + ([prev] if last else [])))


def across(block, same_z):
    pairs = []
    for z in range(2):
        for p in range(2):
            for c in range(2):
                to = z if same_z else 1 - z
                pairs.append((4 * z + 2 * p + c, 4 * to + 2 * c + p))
    return lax.ppermute(block, ("zl", "yp", "core"), pairs)


def shift_x(block, by):
    return lax.ppermute(block, "x", [((i + by) % 4, i) for i in range(4)])


def reduce_half(blocks):
    return jnp.sum(lax.all_to_all(blocks, PLANE, 0, 0, tiled=True).astype(F4), axis=0)


def shards(query, key_new, value_new, key_old, value_old, offset, windows, grad_out):
    zl, yh, yp, xx, core = (lax.axis_index(a) for a in ("zl", "yh", "yp", "x", "core"))

    wins = lax.ppermute(windows, ("yp", "core"), [(0, 0), (1, 2), (2, 1), (3, 3)])
    win = jnp.where(zl == 0, wins[0], wins[1])

    def rows_of(a):
        return jnp.swapaxes(a, 0, 1).reshape(8, 1, HEADS, SUB, HD)

    qd = jnp.concatenate([rows_of(query), rows_of(grad_out)], axis=1)
    qd = lax.all_to_all(qd, COLUMN, 0, 0, tiled=True).reshape(2, 2, 2, 2, HEADS, SUB, HD)

    kv = jnp.stack([jnp.stack([key_new, value_new]), jnp.stack([key_old, value_old])])
    kv = jnp.moveaxis(kv, 3, 0)
    same = across(jnp.where(zl == 0, kv[0], kv[1]), True)
    other = across(jnp.where(zl == 0, kv[1], kv[0]), False)
    same, other, win = lax.optimization_barrier((same, other, win))
    z0 = jnp.where(zl == 0, same, other)
    z1 = jnp.where(zl == 0, other, same)
    slot = (8 * yh + 4 * core + xx) * TOK + jnp.arange(TOK, dtype=jnp.int32)
    upper = (((slot - offset[0]) & (2 * HALF - 1)) >= HALF)[None, :, None]
    old_hi = jnp.where(upper, z0[1], z1[1])
    old_lo = jnp.where(upper, z1[1], z0[1])
    block = jnp.stack([jnp.stack([z0[0], old_lo]), jnp.stack([z1[0], old_hi])])
    far = lax.ppermute(block, "yh", [(0, 1), (1, 0)])
    pair = jnp.stack([jnp.where(yh == 0, block, far), jnp.where(yh == 0, far, block)])
    parts = jnp.stack([pair] + [shift_x(pair, d) for d in (1, 2, 3)])
    own = jnp.stack([lax.dynamic_index_in_dim(parts, (j - xx) & 3, 0, keepdims=False) for j in range(4)], axis=1)
    own = own.reshape(8, *block.shape)
    own, qd = lax.optimization_barrier((own, qd))
    other = lax.ppermute(own, "core", [(0, 1), (1, 0)])

    info = jnp.stack([offset[0], win, 8 * yh + xx, core]).astype(jnp.int32)

    stats = stats_call(info, qd, own, other)
    dq_part, blocks_hi = grads_call(1, False, info, qd, stats, own, other)
    sum_hi = reduce_half(blocks_hi)
    dq, share, others = grads_call(0, True, info, qd, stats, own, other, dq_part)
    others, sum_hi = lax.optimization_barrier((others, sum_hi))
    share = (share + lax.ppermute(others, "core", [(0, 1), (1, 0)])).astype(BF)
    dq = lax.all_to_all(dq, COLUMN, 0, 0, tiled=True)
    dq, share = lax.optimization_barrier((dq, share))
    sum_lo = jnp.sum(lax.all_to_all(share, ("yh", "x"), 0, 0, tiled=True).astype(F4), axis=0)

    grad_query = jnp.swapaxes(dq.reshape(8 * HEADS, SUB, HD), 0, 1).astype(F4)

    r0 = jnp.stack([sum_lo[0], jnp.where(upper, sum_hi[1], sum_lo[1])]).astype(BF)
    r1 = jnp.stack([sum_hi[0], jnp.where(upper, sum_lo[1], sum_hi[1])]).astype(BF)
    same = across(jnp.where(zl == 0, r0, r1), True).astype(F4)
    other = across(jnp.where(zl == 0, r1, r0), False).astype(F4)
    both = jnp.stack([jnp.where(zl == 0, same, other), jnp.where(zl == 0, other, same)], axis=3)
    return (grad_query, both[0, 0], both[0, 1], both[1, 0], both[1, 1])


def solution(mesh):
    fine = Mesh(mesh.devices.reshape(2, 2, 2, 4, 2, 2), ALL)
    tokens = P(ALL, None, None)
    slots = P(("zl", "yh", "yp", "x"), ("zh", "core"), None)
    return jax.shard_map(
        shards,
        mesh=fine,
        in_specs=(tokens, slots, slots, slots, slots, P(), P(("zh", "core")), tokens),
        out_specs=(tokens, slots, slots, slots, slots),
        check_vma=False,
    )
```
